768 devices in a mesh: rep: 16 (over x, z_hi), grp: 48 (over z_lo, y, core).
Axes of the slice: x: 4, y: 8, z: 12 (z_hi: 4, z_lo: 3; z = z_hi * 3 + z_lo), core: 2. Of those that a mesh axis runs over, the one named last changes fastest.
Arguments:
- tokens: bfloat16 [196608, 4608], P(('rep', 'grp')), may hold values from -24 to 24
- key_cotangent: bfloat16 [196608, 512], P(('rep', 'grp')), may hold values from -0.03125 to 0.03125
- weight_codes: bfloat16 [144, 128, 128], P('grp'), may hold values from -6 to 6
- block_scales: bfloat16 [144, 1, 128], P('grp'), may hold values from 0.0059814453 to 0.023925781
- master_weight: float32 [4608, 512], P(('rep', 'grp')), may hold values from -3 to 3
- first_moment: float32 [4608, 512], P(('rep', 'grp')), may hold values from -6 to 6
- second_moment: float32 [4608, 512], P(('rep', 'grp')), may hold values from 0.25 to 4
Outputs:
- projected: bfloat16 [196608, 512], P(('rep', 'grp'))
- new_first: float32 [4608, 512], P(('rep', 'grp'))
- new_second: float32 [4608, 512], P(('rep', 'grp'))
- new_weight: float32 [4608, 512], P(('rep', 'grp'))
The draws below stay inside these ranges and needn't reach their ends.
All inputs are finite; a program needn't handle non-finite values.
Results may differ from the reference program's by a relative error of at most 0.0049.
Values may be sent and summed in bfloat16 or wider, within the bound.
No kernel may reach another device: no remote copies, remote signals or barrier semaphores. Data moves between devices by JAX's collectives and lax.ppermute only.
A program may use at most 64 MiB of HBM per device.

```python
import math
import jax
import jax.numpy as jnp
from jax import lax

DW = 4608
BLK = 128
TOK_DEV = 256
COLS = 512
ROWBLK = 36
COLBLK = 4
TILES = 144
TOKENS = 196608
N_REP = 16
N_GRP = 48


def strengthened(array, rng, source, target, parts, factor):
    owner, partner = [(jnp.arange(array.shape[axis_at]) // (array.shape[axis_at] // parts)).reshape([-1 if axis == axis_at else 1 for axis in range(array.ndim)]) for axis_at in (source, target)]
    chosen = jax.random.permutation(rng, parts)[partner]
    strong = (owner == chosen) | (owner == (partner + parts // 2) % parts)
    return jnp.where(strong, factor * array, array)


def levels(rng, extent, cuts, least, high):
    level = 1.0
    for dim, shards_of in cuts:
        draws = jax.random.uniform(jax.random.fold_in(jax.random.fold_in(rng, 6), dim), (shards_of,), jnp.float32, least / len(cuts), high / len(cuts))
        level = level * jnp.repeat(jnp.exp(draws), extent[dim] // shards_of).reshape((-1,) + (1,) * (len(extent) - 1 - dim))
    return level


def centred(rng, shape, deviation, most, pieces=(), held_as=jnp.bfloat16):
    array = jax.random.normal(rng, shape, jnp.float32) * deviation
    if len(pieces) > 0:
        array = levels(rng, shape, pieces, -0.22, 0.18) * array
    return jnp.clip(array, min=-most, max=most).astype(held_as)


def bell_draw_with(stream_key, shape, scale, most, cuts, heavy, dtype=jnp.bfloat16):
    entries = scale * jax.random.normal(stream_key, shape, jnp.float32)
    if cuts:
        entries = entries * levels(stream_key, shape, cuts, -0.22, 0.18)
    return jnp.clip(strengthened(entries, jax.random.fold_in(stream_key, 3), *heavy), -most, most).astype(dtype)


def setup_inputs(seed: int = 0) -> dict:
    arg_keys = jax.random.split(jax.random.key(seed), 8)
    return {
        "tokens": bell_draw_with(arg_keys[0], (TOKENS, DW), 1.0, 24.0, ((0, 768),), (0, 1, 768, 6.0)),
        "key_cotangent": centred(arg_keys[1], (TOKENS, COLS), (TOKENS ** -0.5), 0.03125, ((0, 768),)),
        "weight_codes": centred(arg_keys[2], (TILES, BLK, BLK), 1.0, 6.0, ((0, 48),)),
        "block_scales": jnp.clip(jnp.exp(math.log(0.023925781) - 1.3862944 * jax.random.uniform(arg_keys[3], (TILES, 1, BLK), jnp.float32) ** levels(arg_keys[3], (TILES, 1, BLK), ((0, 48),), -0.2, 0.2)), 0.0059814453, 0.023925781).astype(jnp.bfloat16),
        "master_weight": centred(arg_keys[4], (DW, COLS), 0.5, 3.0, ((0, 768),), jnp.float32),
        "first_moment": centred(arg_keys[5], (DW, COLS), 1.0, 6.0, ((0, 768),), jnp.float32),
        "second_moment": jnp.clip(jnp.exp(math.log(4.0) - 2.7725887 * jax.random.uniform(arg_keys[6], (DW, COLS), jnp.float32) ** levels(arg_keys[6], (DW, COLS), ((0, 768),), -0.2, 0.2)), 0.25, 4.0),
    }


def add_term(total, pair):
    term = jnp.dot(pair[0].T, pair[1], preferred_element_type=jnp.float32).astype(jnp.bfloat16)
    return (total + lax.optimization_barrier(term).astype(jnp.float32), None)

def reference(tokens, key_cotangent, weight_codes, block_scales, master_weight, first_moment, second_moment):
    tiles = (weight_codes.astype(jnp.float32) * block_scales.astype(jnp.float32)).astype(jnp.bfloat16)
    weights = jnp.transpose(tiles.reshape(ROWBLK, COLBLK, BLK, BLK), (0, 2, 1, 3)).reshape(DW, COLS)
    projected = jnp.dot(tokens, weights, preferred_element_type=jnp.float32).astype(jnp.bfloat16)
    token_blocks = tokens.reshape(N_REP * N_GRP, TOK_DEV, DW)
    cot_blocks = key_cotangent.reshape(N_REP * N_GRP, TOK_DEV, COLS)
    gradient, _ = lax.scan(add_term, jnp.zeros((DW, COLS), jnp.float32), (token_blocks, cot_blocks))
    new_first = 0.9 * first_moment + 0.1 * gradient
    new_second = 0.99 * second_moment + 0.01 * gradient * gradient
    correct_one = 1.0 - 0.9 ** 20
    correct_two = 1.0 - 0.99 ** 20
    update = new_first / correct_one / (jnp.sqrt(new_second / correct_two) + 1e-08)
    new_weight = master_weight - 0.5 * update
    return (projected, new_first, new_second, new_weight)
```

```python
import jax
import jax.numpy as jnp
from jax import lax
from jax.experimental import pallas as pl
from jax.experimental.pallas import tpu as pltpu
from jax.sharding import Mesh, PartitionSpec as P

BETA_ONE = 0.9
BETA_TWO = 0.99
STEP_SIZE = 0.5
EPSILON = 1e-08
CORRECT_ONE = 1.0 - 0.9**20
CORRECT_TWO = 1.0 - 0.99**20
NX, NZH, NZL, NY, NC = 4, 4, 3, 8, 2
AXES = ("x", "zh", "zl", "y", "c")
BF = jnp.bfloat16
F32 = jnp.float32
SLABS = 6


def project_kernel(tokens_ref, tiles_ref, out_ref, weights, sems):
    blk = tiles_ref.shape[-1]
    cbs = out_ref.shape[1] // blk
    rows = weights.shape[0] // SLABS
    per_slab = (rows // blk) * cbs

    def slab(s):
        return weights.at[pl.ds(s * rows, rows)]

    for s in range(SLABS):
        for t in range(s * per_slab, (s + 1) * per_slab):
            owner, i = divmod(t, 3)
            z, q = divmod(owner, NY * NC)
            pltpu.make_async_copy(
                tiles_ref.at[q, z * 3 + i],
                weights.at[pl.ds(t // cbs * blk, blk), pl.ds(t % cbs * blk, blk)],
                sems.at[s],
            ).start()
    total = None
    for s in range(SLABS):
        pltpu.make_async_copy(slab(s), slab(s), sems.at[s]).wait()
        part = jnp.dot(tokens_ref[:, s * rows : (s + 1) * rows], slab(s)[...], preferred_element_type=F32)
        total = part if total is None else total + part
    out_ref[...] = total.astype(out_ref.dtype)


def project(tokens, tiles, columns):
    rows, width = tokens.shape
    return pl.pallas_call(
        project_kernel,
        out_shape=jax.ShapeDtypeStruct((rows, columns), BF),
        in_specs=[pl.BlockSpec(memory_space=pltpu.VMEM), pl.BlockSpec(memory_space=pl.ANY)],
        out_specs=pl.BlockSpec(memory_space=pltpu.VMEM),
        scratch_shapes=[pltpu.VMEM((width, columns), BF), pltpu.SemaphoreType.DMA((SLABS,))],
        compiler_params=pltpu.CompilerParams(vmem_limit_bytes=24 * 2**20),
        cost_estimate=pl.CostEstimate(
            flops=2 * rows * width * columns, bytes_accessed=2 * (rows * width + width * columns), transcendentals=0
        ),
    )(tokens, tiles)


def dot_t(a, b):
    return lax.dot_general(a, b, (((0,), (0,)), ((), ())), preferred_element_type=F32)


def local(tokens, cot, codes, scales, master, first, second):
    width, columns = tokens.shape[1], cot.shape[1]
    x, zl, c = (lax.axis_index(a).astype(jnp.uint32) for a in ("x", "zl", "c"))

    w = (codes.astype(F32) * scales.astype(F32)).astype(BF)
    nz = NZH * NZL
    below = lax.ppermute(w, ("zh", "zl"), [(i, (i + 1) % nz) for i in range(nz)])
    above = lax.ppermute(w, ("zh", "zl"), [(i, (i - 1) % nz) for i in range(nz)])
    cyc = jnp.concatenate([w, above, below, w, above])
    ordered = lax.dynamic_slice_in_dim(cyc, jnp.where(zl == 0, 0, 3 - zl) * w.shape[0], 3 * w.shape[0])
    tiles = lax.all_gather(ordered, ("y", "c"), axis=0)

    chunk, half = width // NX, columns // 2
    swap = [(0, 1), (1, 0)]
    mine_on, their_on = x + 1 + 2 * c, x + 3 - 2 * c

    def part(j):
        return lax.dynamic_slice_in_dim(tokens, (j & (NX - 1)) * chunk, chunk, axis=1)

    theirs = lax.ppermute(jnp.stack([part(x + 2), part(their_on), part(x)]), "c", swap)
    cot_theirs = lax.ppermute(cot, "c", swap)
    near = [lax.dynamic_slice_in_dim(k, c * half, half, axis=1) for k in (cot, cot_theirs)]
    far = [lax.dynamic_slice_in_dim(k, (1 - c) * half, half, axis=1) for k in (cot, cot_theirs)]

    def term(k, j, cots):
        return dot_t(part(j), cots[0]) + dot_t(theirs[k], cots[1])

    straight = [(2 * i + d, 2 * ((i + 1 - 2 * d) % NX) + d) for i in range(NX) for d in range(2)]
    crossed = [(2 * i + d, 2 * ((i + 1 - 2 * d) % NX) + 1 - d) for i in range(NX) for d in range(2)]
    two_on = lax.ppermute(term(0, x + 2, near).astype(BF), ("x", "c"), straight)
    one_far = lax.ppermute(term(1, mine_on, far).astype(BF), ("x", "c"), crossed)
    one_near = (term(1, mine_on, near) + two_on.astype(F32)).astype(BF)
    one_near = lax.ppermute(one_near, ("x", "c"), straight)
    summed = (term(2, x, near) + one_far.astype(F32) + one_near.astype(F32)).astype(BF)

    rows = chunk // (nz * NY)
    by_y = summed.reshape(nz, NY, rows, half).transpose(1, 0, 2, 3)
    by_y = lax.all_to_all(by_y, "y", 0, 0, tiled=True)
    by_z = jnp.sum(by_y.astype(F32), axis=0).astype(BF).reshape(nz * NC, rows // NC, half)
    by_z = lax.all_to_all(by_z, ("zh", "zl", "c"), 0, 0, tiled=True)
    gradient = jnp.sum(by_z.astype(F32).reshape(nz, NC, rows // NC, half), axis=0)
    gradient = gradient.transpose(1, 0, 2).reshape(rows // NC, columns)

    projected = project(tokens, tiles, columns)
    new_first = BETA_ONE * first + (1.0 - BETA_ONE) * gradient
    new_second = BETA_TWO * second + (1.0 - BETA_TWO) * gradient * gradient
    update = new_first / CORRECT_ONE / (jnp.sqrt(new_second / CORRECT_TWO) + EPSILON)
    new_weight = master - STEP_SIZE * update
    return projected, new_first, new_second, new_weight


def solution(mesh):
    fine = Mesh(mesh.devices.reshape(NX, NZH, NZL, NY, NC), AXES)
    rows = P(AXES, None)
    tiles = P(("zl", "y", "c"), None, None)
    return jax.shard_map(
        local,
        mesh=fine,
        in_specs=(rows, rows, tiles, tiles, rows, rows, rows),
        out_specs=(rows, rows, rows, rows),
        check_vma=False,
    )
```

```python
import jax
import jax.numpy as jnp
from jax import lax
from jax.experimental import pallas as pl
from jax.experimental.pallas import tpu as pltpu
from jax.sharding import Mesh, PartitionSpec as P

BETA_ONE = 0.9
BETA_TWO = 0.99
STEP_SIZE = 0.5
EPSILON = 1e-08
CORRECT_ONE = 1.0 - 0.9**20
CORRECT_TWO = 1.0 - 0.99**20
NX, NZH, NZL, NY, NC = 4, 4, 3, 8, 2
AXES = ("x", "zh", "zl", "y", "c")
BF = jnp.bfloat16
F32 = jnp.float32
SLABS = 6


def project_kernel(tokens_hbm, tiles_ref, out_ref, tokens_ref, weights, sems, tokens_sem):
    blk = tiles_ref.shape[-1]
    cbs = out_ref.shape[1] // blk
    rows = weights.shape[0] // SLABS
    per_slab = (rows // blk) * cbs

    def slab(s):
        return weights.at[pl.ds(s * rows, rows)]

    whole = pltpu.make_async_copy(tokens_hbm, tokens_ref, tokens_sem)
    whole.start()
    for s in range(SLABS):
        for t in range(s * per_slab, (s + 1) * per_slab):
            owner, i = divmod(t, 3)
            z, q = divmod(owner, NY * NC)
            pltpu.make_async_copy(
                tiles_ref.at[q, z * 3 + i],
                weights.at[pl.ds(t // cbs * blk, blk), pl.ds(t % cbs * blk, blk)],
                sems.at[s],
            ).start()
    whole.wait()
    total = None
    for s in range(SLABS):
        pltpu.make_async_copy(slab(s), slab(s), sems.at[s]).wait()
        part = jnp.dot(tokens_ref[:, s * rows : (s + 1) * rows], slab(s)[...], preferred_element_type=F32)
        total = part if total is None else total + part
    out_ref[...] = total.astype(out_ref.dtype)


def project(tokens, tiles, columns):
    rows, width = tokens.shape
    return pl.pallas_call(
        project_kernel,
        out_shape=jax.ShapeDtypeStruct((rows, columns), BF),
        in_specs=[pl.BlockSpec(memory_space=pl.ANY), pl.BlockSpec(memory_space=pl.ANY)],
        out_specs=pl.BlockSpec(memory_space=pltpu.VMEM),
        scratch_shapes=[
            pltpu.VMEM((rows, width), BF),
            pltpu.VMEM((width, columns), BF),
            pltpu.SemaphoreType.DMA((SLABS,)),
            pltpu.SemaphoreType.DMA,
        ],
        compiler_params=pltpu.CompilerParams(vmem_limit_bytes=60 * 2**20),
        cost_estimate=pl.CostEstimate(
            flops=2 * rows * width * columns, bytes_accessed=2 * (rows * width + width * columns), transcendentals=0
        ),
    )(tokens, tiles)


def thirds_kernel(zl_ref, own, above, below, after, out):
    size = own.shape[0]
    for k, third in enumerate((own, above, below)):
        at = zl_ref[0] + k
        at = jnp.where(at >= NZL, at - NZL, at)
        out[pl.ds(at * size, size)] = third[...]


def in_z_order(zl, own, above, below, after):
    vmem = pl.BlockSpec(memory_space=pltpu.VMEM)
    return pl.pallas_call(
        thirds_kernel,
        out_shape=jax.ShapeDtypeStruct((NZL * own.shape[0], *own.shape[1:]), BF),
        in_specs=[pl.BlockSpec(memory_space=pltpu.SMEM), vmem, vmem, vmem, pl.BlockSpec(memory_space=pl.ANY)],
        out_specs=vmem,
        cost_estimate=pl.CostEstimate(flops=0, bytes_accessed=4 * NZL * own.size, transcendentals=0),
    )(zl, own, above, below, after)


def adam_kernel(terms, master, first, second, after, new_first, new_second, new_weight):
    half = terms.shape[-1]
    total = jnp.sum(terms[...].astype(F32), axis=0)
    for k in range(NC):
        at = slice(k * half, (k + 1) * half)
        gradient = total[k]
        one = BETA_ONE * first[:, at] + (1.0 - BETA_ONE) * gradient
        two = BETA_TWO * second[:, at] + (1.0 - BETA_TWO) * gradient * gradient
        new_first[:, at] = one
        new_second[:, at] = two
        new_weight[:, at] = master[:, at] - STEP_SIZE * (
            one / CORRECT_ONE / (jnp.sqrt(two / CORRECT_TWO) + EPSILON)
        )


def adam(terms, master, first, second, after):
    vmem = pl.BlockSpec(memory_space=pltpu.VMEM)
    shape = jax.ShapeDtypeStruct(master.shape, F32)
    return pl.pallas_call(
        adam_kernel,
        out_shape=(shape, shape, shape),
        in_specs=[vmem] * 4 + [pl.BlockSpec(memory_space=pl.ANY)],
        out_specs=(vmem, vmem, vmem),
        cost_estimate=pl.CostEstimate(flops=20 * master.size, bytes_accessed=24 * master.size + 2 * terms.size, transcendentals=0),
    )(terms, master, first, second, after)


def dot_t(a, b):
    return lax.dot_general(a, b, (((0,), (0,)), ((), ())), preferred_element_type=F32)


def local(tokens, cot, codes, scales, master, first, second):
    width, columns = tokens.shape[1], cot.shape[1]
    x, zl, c = (lax.axis_index(a).astype(jnp.uint32) for a in ("x", "zl", "c"))
    nz = NZH * NZL
    swap = [(0, 1), (1, 0)]
    z_up = [(i, (i + 1) % nz) for i in range(nz)]
    z_down = [(i, (i - 1) % nz) for i in range(nz)]

    theirs = lax.ppermute(tokens, "c", swap)
    cot_theirs = lax.ppermute(cot, "c", swap)

    w = (codes.astype(F32) * scales.astype(F32)).astype(BF)
    below = lax.ppermute(w, ("zh", "zl"), z_up)
    above = lax.ppermute(w, ("zh", "zl"), z_down)

    chunk, half = width // NX, columns // 2
    on = x + 1 + 2 * c

    def part(k, j):
        return lax.dynamic_slice_in_dim(k, (j & (NX - 1)) * chunk, chunk, axis=1)

    near = [lax.dynamic_slice_in_dim(k, c * half, half, axis=1) for k in (cot, cot_theirs)]
    far = [lax.dynamic_slice_in_dim(k, (1 - c) * half, half, axis=1) for k in (cot, cot_theirs)]

    def term(j, cots):
        return dot_t(part(tokens, j), cots[0]) + dot_t(part(theirs, j), cots[1])

    straight = [(2 * i + d, 2 * ((i + 1 - 2 * d) % NX) + d) for i in range(NX) for d in range(2)]
    crossed = [(2 * i + d, 2 * ((i + 1 - 2 * d) % NX) + 1 - d) for i in range(NX) for d in range(2)]
    two_on = term(x + 2, near).astype(BF)
    tiles = in_z_order(zl.astype(jnp.int32).reshape(1), w, above, below, two_on)
    tiles = lax.all_gather(tiles, ("y", "c"), axis=0)
    two_on = lax.ppermute(two_on, ("x", "c"), straight)
    one_far = lax.ppermute(term(on, far).astype(BF), ("x", "c"), crossed)
    one_near = (term(on, near) + two_on.astype(F32)).astype(BF)
    one_near = lax.ppermute(one_near, ("x", "c"), straight)
    summed = (term(x, near) + one_far.astype(F32) + one_near.astype(F32)).astype(BF)

    rows = chunk // (nz * NY)
    thirds = summed.reshape(NZH, NZL, NY * rows, half)

    def third(j):
        return lax.dynamic_index_in_dim(thirds, jnp.where(j > 2, j - 3, j), axis=1, keepdims=False)

    up = lax.ppermute(third(zl + 1), ("zh", "zl"), z_up)
    down = lax.ppermute(third(zl + 2), ("zh", "zl"), z_down)
    by_z = (third(zl).astype(F32) + up.astype(F32) + down.astype(F32)).astype(BF)
    last = by_z.reshape(NZH * NY * NC, rows // NC, half)
    last = lax.all_to_all(last, ("zh", "y", "c"), 0, 0, tiled=True)
    last = last.reshape(NZH * NY, NC, rows // NC, half)

    projected = project(tokens, tiles, columns)
    return projected, *adam(last, master, first, second, projected)


def solution(mesh):
    fine = Mesh(mesh.devices.reshape(NX, NZH, NZL, NY, NC), AXES)
    rows = P(AXES, None)
    tiles = P(("zl", "y", "c"), None, None)
    return jax.shard_map(
        local,
        mesh=fine,
        in_specs=(rows, rows, tiles, tiles, rows, rows, rows),
        out_specs=(rows, rows, rows, rows),
        check_vma=False,
    )
```

```python
import functools

import jax
import jax.numpy as jnp
from jax import lax
from jax.experimental import pallas as pl
from jax.experimental.pallas import tpu as pltpu
from jax.sharding import Mesh, PartitionSpec as P

BETA_ONE = 0.9
BETA_TWO = 0.99
STEP_SIZE = 0.5
EPSILON = 1e-08
CORRECT_ONE = 1.0 - 0.9**20
CORRECT_TWO = 1.0 - 0.99**20
NX, NZH, NZL, NY, NC = 4, 4, 3, 8, 2
AXES = ("x", "zh", "zl", "y", "c")
BF = jnp.bfloat16
F32 = jnp.float32
SLABS = 6


def project_kernel(tokens_hbm, tiles_ref, out_ref, tokens_ref, weights, sems, tokens_sem):
    blk = tiles_ref.shape[-1]
    cbs = out_ref.shape[1] // blk
    rows = weights.shape[0] // SLABS
    per_slab = (rows // blk) * cbs

    def slab(s):
        return weights.at[pl.ds(s * rows, rows)]

    whole = pltpu.make_async_copy(tokens_hbm, tokens_ref, tokens_sem)
    whole.start()
    for s in range(SLABS):
        for t in range(s * per_slab, (s + 1) * per_slab):
            owner, i = divmod(t, 3)
            z, q = divmod(owner, NY * NC)
            pltpu.make_async_copy(
                tiles_ref.at[q, z * 3 + i],
                weights.at[pl.ds(t // cbs * blk, blk), pl.ds(t % cbs * blk, blk)],
                sems.at[s],
            ).start()
    whole.wait()
    total = None
    for s in range(SLABS):
        pltpu.make_async_copy(slab(s), slab(s), sems.at[s]).wait()
        part = jnp.dot(tokens_ref[:, s * rows : (s + 1) * rows], slab(s)[...], preferred_element_type=F32)
        total = part if total is None else total + part
    out_ref[...] = total.astype(out_ref.dtype)


def project(tokens, tiles, columns):
    rows, width = tokens.shape
    return pl.pallas_call(
        project_kernel,
        out_shape=jax.ShapeDtypeStruct((rows, columns), BF),
        in_specs=[pl.BlockSpec(memory_space=pl.ANY), pl.BlockSpec(memory_space=pl.ANY)],
        out_specs=pl.BlockSpec(memory_space=pltpu.VMEM),
        scratch_shapes=[
            pltpu.VMEM((rows, width), BF),
            pltpu.VMEM((width, columns), BF),
            pltpu.SemaphoreType.DMA((SLABS,)),
            pltpu.SemaphoreType.DMA,
        ],
        compiler_params=pltpu.CompilerParams(vmem_limit_bytes=60 * 2**20),
        cost_estimate=pl.CostEstimate(
            flops=2 * rows * width * columns, bytes_accessed=2 * (rows * width + width * columns), transcendentals=0
        ),
    )(tokens, tiles)


def thirds_kernel(zl_ref, own, above, below, after, out):
    size = own.shape[0]
    for k, third in enumerate((own, above, below)):
        at = zl_ref[0] + k
        at = jnp.where(at >= NZL, at - NZL, at)
        out[pl.ds(at * size, size)] = third[...]


def in_z_order(zl, own, above, below, after):
    vmem = pl.BlockSpec(memory_space=pltpu.VMEM)
    return pl.pallas_call(
        thirds_kernel,
        out_shape=jax.ShapeDtypeStruct((NZL * own.shape[0], *own.shape[1:]), BF),
        in_specs=[pl.BlockSpec(memory_space=pltpu.SMEM), vmem, vmem, vmem, pl.BlockSpec(memory_space=pl.ANY)],
        out_specs=vmem,
        compiler_params=pltpu.CompilerParams(vmem_limit_bytes=60 * 2**20),
        cost_estimate=pl.CostEstimate(flops=0, bytes_accessed=4 * NZL * own.size, transcendentals=0),
    )(zl, own, above, below, after)


def adam_kernel(terms, master, first, second, after, new_first, new_second, new_weight):
    half = terms.shape[-1]
    total = jnp.sum(terms[...].astype(F32), axis=0)
    for k in range(NC):
        at = slice(k * half, (k + 1) * half)
        gradient = total[k]
        one = BETA_ONE * first[:, at] + (1.0 - BETA_ONE) * gradient
        two = BETA_TWO * second[:, at] + (1.0 - BETA_TWO) * gradient * gradient
        new_first[:, at] = one
        new_second[:, at] = two
        new_weight[:, at] = master[:, at] - STEP_SIZE * (
            one / CORRECT_ONE / (jnp.sqrt(two / CORRECT_TWO) + EPSILON)
        )


def adam(terms, master, first, second, after):
    vmem = pl.BlockSpec(memory_space=pltpu.VMEM)
    shape = jax.ShapeDtypeStruct(master.shape, F32)
    return pl.pallas_call(
        adam_kernel,
        out_shape=(shape, shape, shape),
        in_specs=[vmem] * 4 + [pl.BlockSpec(memory_space=pl.ANY)],
        out_specs=(vmem, vmem, vmem),
        cost_estimate=pl.CostEstimate(flops=20 * master.size, bytes_accessed=24 * master.size + 2 * terms.size, transcendentals=0),
    )(terms, master, first, second, after)


def term_kernel(plan, where, tokens, theirs, cot, cot_theirs, after, *rest):
    outs, (lhs, rhs, sems) = rest[: len(plan)], rest[len(plan) :]
    rows, chunk = lhs.shape[1] // 2, lhs.shape[2]
    half = outs[0].shape[1]
    chunks = sorted({p[0] for p in plan})

    def copies(k):
        columns = pl.ds(pl.multiple_of(where[chunks[k]] * chunk, 128), chunk)
        return [
            pltpu.make_async_copy(source.at[:, columns], lhs.at[k, pl.ds(d * rows, rows)], sems.at[k, d])
            for d, source in enumerate((tokens, theirs))
        ]

    for k in range(len(chunks)):
        for copy in copies(k):
            copy.start()
    arrived = set()
    for out, (which, side, kind) in zip(outs, plan):
        columns = pl.ds(pl.multiple_of(where[side] * half, 128), half)
        rhs[:rows] = cot[:, columns]
        rhs[rows:] = cot_theirs[:, columns]
        k = chunks.index(which)
        if k not in arrived:
            arrived.add(k)
            for copy in copies(k):
                copy.wait()
        value = lax.dot_general(lhs[k], rhs[...], (((0,), (0,)), ((), ())), preferred_element_type=F32)
        out[...] = value.astype(kind)


def terms(plan, where, tokens, theirs, cot, cot_theirs, after):
    rows, chunk, half = tokens.shape[0], tokens.shape[1] // NX, cot.shape[1] // 2
    vmem, hbm = pl.BlockSpec(memory_space=pltpu.VMEM), pl.BlockSpec(memory_space=pl.ANY)
    count = len({p[0] for p in plan})
    return pl.pallas_call(
        functools.partial(term_kernel, plan),
        out_shape=[jax.ShapeDtypeStruct((chunk, half), p[2]) for p in plan],
        in_specs=[pl.BlockSpec(memory_space=pltpu.SMEM), hbm, hbm, vmem, vmem, hbm],
        out_specs=[vmem] * len(plan),
        scratch_shapes=[
            pltpu.VMEM((count, 2 * rows, chunk), BF),
            pltpu.VMEM((2 * rows, half), BF),
            pltpu.SemaphoreType.DMA((count, 2)),
        ],
        compiler_params=pltpu.CompilerParams(vmem_limit_bytes=60 * 2**20),
        cost_estimate=pl.CostEstimate(
            flops=4 * rows * chunk * half * len(plan), bytes_accessed=4 * rows * chunk * count, transcendentals=0
        ),
    )(where, tokens, theirs, cot, cot_theirs, after)


def local(tokens, cot, codes, scales, master, first, second):
    width, columns = tokens.shape[1], cot.shape[1]
    x, zl, c = (lax.axis_index(a).astype(jnp.uint32) for a in ("x", "zl", "c"))
    nz = NZH * NZL
    swap = [(0, 1), (1, 0)]
    z_up = [(i, (i + 1) % nz) for i in range(nz)]
    z_down = [(i, (i - 1) % nz) for i in range(nz)]

    theirs = lax.ppermute(tokens, "c", swap)
    cot_theirs = lax.ppermute(cot, "c", swap)

    w = (codes.astype(F32) * scales.astype(F32)).astype(BF)
    below = lax.ppermute(w, ("zh", "zl"), z_up)
    above = lax.ppermute(w, ("zh", "zl"), z_down)

    chunk, half = width // NX, columns // 2
    on = x + 1 + 2 * c

    where = jnp.stack([(x + 2) & (NX - 1), on & (NX - 1), x, c, 1 - c]).astype(jnp.int32)
    both = (where, tokens, theirs, cot, cot_theirs)
    TWO, ONE, HERE, NEAR, FAR = range(5)
    straight = [(2 * i + d, 2 * ((i + 1 - 2 * d) % NX) + d) for i in range(NX) for d in range(2)]
    crossed = [(2 * i + d, 2 * ((i + 1 - 2 * d) % NX) + 1 - d) for i in range(NX) for d in range(2)]
    (two_on,) = terms([(TWO, NEAR, BF)], *both, cot)
    tiles = in_z_order(zl.astype(jnp.int32).reshape(1), w, above, below, two_on)
    tiles = lax.all_gather(tiles, ("y", "c"), axis=0)
    (one_far,) = terms([(ONE, FAR, BF)], *both, two_on)
    one_near, here = terms([(ONE, NEAR, F32), (HERE, NEAR, F32)], *both, one_far)
    two_on = lax.ppermute(two_on, ("x", "c"), straight)
    one_far = lax.ppermute(one_far, ("x", "c"), crossed)
    one_near = lax.ppermute((one_near + two_on.astype(F32)).astype(BF), ("x", "c"), straight)
    summed = (here + one_far.astype(F32) + one_near.astype(F32)).astype(BF)

    rows = chunk // (nz * NY)
    thirds = summed.reshape(NZH, NZL, NY * rows, half)

    def third(j):
        return lax.dynamic_index_in_dim(thirds, jnp.where(j > 2, j - 3, j), axis=1, keepdims=False)

    up = lax.ppermute(third(zl + 1), ("zh", "zl"), z_up)
    down = lax.ppermute(third(zl + 2), ("zh", "zl"), z_down)
    by_z = (third(zl).astype(F32) + up.astype(F32) + down.astype(F32)).astype(BF)
    last = by_z.reshape(NZH * NY * NC, rows // NC, half)
    last = lax.all_to_all(last, ("zh", "y", "c"), 0, 0, tiled=True)
    last = last.reshape(NZH * NY, NC, rows // NC, half)

    projected = project(tokens, tiles, columns)
    return projected, *adam(last, master, first, second, projected)


def solution(mesh):
    fine = Mesh(mesh.devices.reshape(NX, NZH, NZL, NY, NC), AXES)
    rows = P(AXES, None)
    tiles = P(("zl", "y", "c"), None, None)
    return jax.shard_map(
        local,
        mesh=fine,
        in_specs=(rows, rows, tiles, tiles, rows, rows, rows),
        out_specs=(rows, rows, rows, rows),
        check_vma=False,
    )
```

```python
import functools

import jax
import jax.numpy as jnp
from jax import lax
from jax.experimental import pallas as pl
from jax.experimental.pallas import tpu as pltpu
from jax.sharding import Mesh, PartitionSpec as P

BETA_ONE = 0.9
BETA_TWO = 0.99
STEP_SIZE = 0.5
EPSILON = 1e-08
CORRECT_ONE = 1.0 - 0.9**20
CORRECT_TWO = 1.0 - 0.99**20
NX, NZH, NZL, NY, NC = 4, 4, 3, 8, 2
AXES = ("x", "zh", "zl", "y", "c")
BF = jnp.bfloat16
F32 = jnp.float32
SLABS = 6


def project_kernel(tokens_hbm, tiles_ref, out_ref, tokens_ref, weights, sems, tokens_sem):
    blk = tiles_ref.shape[-1]
    cbs = out_ref.shape[1] // blk
    rows = weights.shape[0] // SLABS
    per_slab = (rows // blk) * cbs

    def slab(s):
        return weights.at[pl.ds(s * rows, rows)]

    whole = pltpu.make_async_copy(tokens_hbm, tokens_ref, tokens_sem)
    whole.start()
    for s in range(SLABS):
        for t in range(s * per_slab, (s + 1) * per_slab):
            owner, i = divmod(t, 3)
            z, q = divmod(owner, NY * NC)
            pltpu.make_async_copy(
                tiles_ref.at[q, z * 3 + i],
                weights.at[pl.ds(t // cbs * blk, blk), pl.ds(t % cbs * blk, blk)],
                sems.at[s],
            ).start()
    whole.wait()
    total = None
    for s in range(SLABS):
        pltpu.make_async_copy(slab(s), slab(s), sems.at[s]).wait()
        part = jnp.dot(tokens_ref[:, s * rows : (s + 1) * rows], slab(s)[...], preferred_element_type=F32)
        total = part if total is None else total + part
    out_ref[...] = total.astype(out_ref.dtype)


def project(tokens, tiles, columns):
    rows, width = tokens.shape
    return pl.pallas_call(
        project_kernel,
        out_shape=jax.ShapeDtypeStruct((rows, columns), BF),
        in_specs=[pl.BlockSpec(memory_space=pl.ANY), pl.BlockSpec(memory_space=pl.ANY)],
        out_specs=pl.BlockSpec(memory_space=pltpu.VMEM),
        scratch_shapes=[
            pltpu.VMEM((rows, width), BF),
            pltpu.VMEM((width, columns), BF),
            pltpu.SemaphoreType.DMA((SLABS,)),
            pltpu.SemaphoreType.DMA,
        ],
        compiler_params=pltpu.CompilerParams(vmem_limit_bytes=60 * 2**20),
        cost_estimate=pl.CostEstimate(
            flops=2 * rows * width * columns, bytes_accessed=2 * (rows * width + width * columns), transcendentals=0
        ),
    )(tokens, tiles)


def thirds_kernel(zl_ref, own, above, below, after, out):
    size = own.shape[0]
    for k, third in enumerate((own, above, below)):
        at = zl_ref[0] + k
        at = jnp.where(at >= NZL, at - NZL, at)
        out[pl.ds(at * size, size)] = third[...]


def in_z_order(zl, own, above, below, after):
    vmem = pl.BlockSpec(memory_space=pltpu.VMEM)
    return pl.pallas_call(
        thirds_kernel,
        out_shape=jax.ShapeDtypeStruct((NZL * own.shape[0], *own.shape[1:]), BF),
        in_specs=[pl.BlockSpec(memory_space=pltpu.SMEM), vmem, vmem, vmem, pl.BlockSpec(memory_space=pl.ANY)],
        out_specs=vmem,
        compiler_params=pltpu.CompilerParams(vmem_limit_bytes=60 * 2**20),
        cost_estimate=pl.CostEstimate(flops=0, bytes_accessed=4 * NZL * own.size, transcendentals=0),
    )(zl, own, above, below, after)


def adam_kernel(terms, master, first, second, after, new_first, new_second, new_weight):
    half = terms.shape[-1]
    total = jnp.sum(terms[...].astype(F32), axis=0)
    for k in range(NC):
        at = slice(k * half, (k + 1) * half)
        gradient = total[k]
        one = BETA_ONE * first[:, at] + (1.0 - BETA_ONE) * gradient
        two = BETA_TWO * second[:, at] + (1.0 - BETA_TWO) * gradient * gradient
        new_first[:, at] = one
        new_second[:, at] = two
        new_weight[:, at] = master[:, at] - STEP_SIZE * (
            one / CORRECT_ONE / (jnp.sqrt(two / CORRECT_TWO) + EPSILON)
        )


def adam(terms, master, first, second, after):
    vmem = pl.BlockSpec(memory_space=pltpu.VMEM)
    shape = jax.ShapeDtypeStruct(master.shape, F32)
    return pl.pallas_call(
        adam_kernel,
        out_shape=(shape, shape, shape),
        in_specs=[vmem] * 4 + [pl.BlockSpec(memory_space=pl.ANY)],
        out_specs=(vmem, vmem, vmem),
        cost_estimate=pl.CostEstimate(flops=20 * master.size, bytes_accessed=24 * master.size + 2 * terms.size, transcendentals=0),
    )(terms, master, first, second, after)


def term_kernel(plan, where, tokens, theirs, cot, cot_theirs, after, *rest):
    outs, (lhs, rhs, sems) = rest[: len(plan)], rest[len(plan) :]
    rows, chunk = lhs.shape[1] // 2, lhs.shape[2]
    half = outs[0].shape[1]
    chunks = sorted({p[0] for p in plan})

    def copies(k):
        columns = pl.ds(pl.multiple_of(where[chunks[k]] * chunk, 128), chunk)
        return [
            pltpu.make_async_copy(source.at[:, columns], lhs.at[k, pl.ds(d * rows, rows)], sems.at[k, d])
            for d, source in enumerate((tokens, theirs))
        ]

    for k in range(len(chunks)):
        for copy in copies(k):
            copy.start()
    arrived = set()
    for out, (which, side, kind) in zip(outs, plan):
        columns = pl.ds(pl.multiple_of(where[side] * half, 128), half)
        rhs[:rows] = cot[:, columns]
        rhs[rows:] = cot_theirs[:, columns]
        k = chunks.index(which)
        if k not in arrived:
            arrived.add(k)
            for copy in copies(k):
                copy.wait()
        value = lax.dot_general(lhs[k], rhs[...], (((0,), (0,)), ((), ())), preferred_element_type=F32)
        out[...] = value.astype(kind)


def terms(plan, where, tokens, theirs, cot, cot_theirs, after):
    rows, chunk, half = tokens.shape[0], tokens.shape[1] // NX, cot.shape[1] // 2
    vmem, hbm = pl.BlockSpec(memory_space=pltpu.VMEM), pl.BlockSpec(memory_space=pl.ANY)
    count = len({p[0] for p in plan})
    return pl.pallas_call(
        functools.partial(term_kernel, plan),
        out_shape=[jax.ShapeDtypeStruct((chunk, half), p[2]) for p in plan],
        in_specs=[pl.BlockSpec(memory_space=pltpu.SMEM), hbm, hbm, vmem, vmem, hbm],
        out_specs=[vmem] * len(plan),
        scratch_shapes=[
            pltpu.VMEM((count, 2 * rows, chunk), BF),
            pltpu.VMEM((2 * rows, half), BF),
            pltpu.SemaphoreType.DMA((count, 2)),
        ],
        compiler_params=pltpu.CompilerParams(vmem_limit_bytes=60 * 2**20),
        cost_estimate=pl.CostEstimate(
            flops=4 * rows * chunk * half * len(plan), bytes_accessed=4 * rows * chunk * count, transcendentals=0
        ),
    )(where, tokens, theirs, cot, cot_theirs, after)


def local(tokens, cot, codes, scales, master, first, second):
    width, columns = tokens.shape[1], cot.shape[1]
    x, zl, c = (lax.axis_index(a).astype(jnp.uint32) for a in ("x", "zl", "c"))
    nz = NZH * NZL
    swap = [(0, 1), (1, 0)]
    z_up = [(i, (i + 1) % nz) for i in range(nz)]
    z_down = [(i, (i - 1) % nz) for i in range(nz)]

    theirs = lax.ppermute(tokens, "c", swap)
    cot_theirs = lax.ppermute(cot, "c", swap)

    w = (codes.astype(F32) * scales.astype(F32)).astype(BF)
    below = lax.ppermute(w, ("zh", "zl"), z_up)
    above = lax.ppermute(w, ("zh", "zl"), z_down)

    chunk, half = width // NX, columns // 2
    on = x + 1 + 2 * c

    where = jnp.stack([(x + 2) & (NX - 1), on & (NX - 1), x, c, 1 - c]).astype(jnp.int32)
    both = (where, tokens, theirs, cot, cot_theirs)
    TWO, ONE, HERE, NEAR, FAR = range(5)
    straight = [(2 * i + d, 2 * ((i + 1 - 2 * d) % NX) + d) for i in range(NX) for d in range(2)]
    crossed = [(2 * i + d, 2 * ((i + 1 - 2 * d) % NX) + 1 - d) for i in range(NX) for d in range(2)]
    (two_on,) = terms([(TWO, NEAR, BF)], *both, cot)
    tiles = in_z_order(zl.astype(jnp.int32).reshape(1), w, above, below, two_on)
    tiles = lax.all_gather(tiles, ("y", "c"), axis=0)
    (one_far,) = terms([(ONE, FAR, BF)], *both, two_on)
    (one_near,) = terms([(ONE, NEAR, F32)], *both, one_far)
    two_on = lax.ppermute(two_on, ("x", "c"), straight)
    one_far = lax.ppermute(one_far, ("x", "c"), crossed)
    one_near = (one_near + two_on.astype(F32)).astype(BF)
    (here,) = terms([(HERE, NEAR, F32)], *both, one_near)
    one_near = lax.ppermute(one_near, ("x", "c"), straight)
    summed = (here + one_far.astype(F32) + one_near.astype(F32)).astype(BF)

    rows = chunk // (nz * NY)
    thirds = summed.reshape(NZH, NZL, NY * rows, half)

    def third(j):
        return lax.dynamic_index_in_dim(thirds, jnp.where(j > 2, j - 3, j), axis=1, keepdims=False)

    up = lax.ppermute(third(zl + 1), ("zh", "zl"), z_up)
    down = lax.ppermute(third(zl + 2), ("zh", "zl"), z_down)
    by_z = (third(zl).astype(F32) + up.astype(F32) + down.astype(F32)).astype(BF)
    last = by_z.reshape(NZH * NY * NC, rows // NC, half)
    last = lax.all_to_all(last, ("zh", "y", "c"), 0, 0, tiled=True)
    last = last.reshape(NZH * NY, NC, rows // NC, half)

    projected = project(tokens, tiles, columns)
    return projected, *adam(last, master, first, second, projected)


def solution(mesh):
    fine = Mesh(mesh.devices.reshape(NX, NZH, NZL, NY, NC), AXES)
    rows = P(AXES, None)
    tiles = P(("zl", "y", "c"), None, None)
    return jax.shard_map(
        local,
        mesh=fine,
        in_specs=(rows, rows, tiles, tiles, rows, rows, rows),
        out_specs=(rows, rows, rows, rows),
        check_vma=False,
    )
```

```python
import functools

import jax
import jax.numpy as jnp
from jax import lax
from jax.experimental import pallas as pl
from jax.experimental.pallas import tpu as pltpu
from jax.sharding import Mesh, PartitionSpec as P

BETA_ONE = 0.9
BETA_TWO = 0.99
STEP_SIZE = 0.5
EPSILON = 1e-08
CORRECT_ONE = 1.0 - 0.9**20
CORRECT_TWO = 1.0 - 0.99**20
NX, NZH, NZL, NY, NC = 4, 4, 3, 8, 2
AXES = ("x", "zh", "zl", "y", "c")
BF = jnp.bfloat16
F32 = jnp.float32
SLABS = 6


def project_kernel(tokens_hbm, tiles_ref, out_ref, tokens_ref, weights, sems, tokens_sem):
    blk = tiles_ref.shape[-1]
    cbs = out_ref.shape[1] // blk
    rows = weights.shape[0] // SLABS
    per_slab = (rows // blk) * cbs

    def slab(s):
        return weights.at[pl.ds(s * rows, rows)]

    whole = pltpu.make_async_copy(tokens_hbm, tokens_ref, tokens_sem)
    whole.start()
    for s in range(SLABS):
        for t in range(s * per_slab, (s + 1) * per_slab):
            owner, i = divmod(t, 3)
            z, q = divmod(owner, NY * NC)
            pltpu.make_async_copy(
                tiles_ref.at[q, z * 3 + i],
                weights.at[pl.ds(t // cbs * blk, blk), pl.ds(t % cbs * blk, blk)],
                sems.at[s],
            ).start()
    whole.wait()
    total = None
    for s in range(SLABS):
        pltpu.make_async_copy(slab(s), slab(s), sems.at[s]).wait()
        part = jnp.dot(tokens_ref[:, s * rows : (s + 1) * rows], slab(s)[...], preferred_element_type=F32)
        total = part if total is None else total + part
    out_ref[...] = total.astype(out_ref.dtype)


def project(tokens, tiles, columns):
    rows, width = tokens.shape
    return pl.pallas_call(
        project_kernel,
        out_shape=jax.ShapeDtypeStruct((rows, columns), BF),
        in_specs=[pl.BlockSpec(memory_space=pl.ANY), pl.BlockSpec(memory_space=pl.ANY)],
        out_specs=pl.BlockSpec(memory_space=pltpu.VMEM),
        scratch_shapes=[
            pltpu.VMEM((rows, width), BF),
            pltpu.VMEM((width, columns), BF),
            pltpu.SemaphoreType.DMA((SLABS,)),
            pltpu.SemaphoreType.DMA,
        ],
        compiler_params=pltpu.CompilerParams(vmem_limit_bytes=60 * 2**20),
        cost_estimate=pl.CostEstimate(
            flops=2 * rows * width * columns, bytes_accessed=2 * (rows * width + width * columns), transcendentals=0
        ),
    )(tokens, tiles)


def thirds_kernel(zl_ref, own, above, below, after, out):
    size = own.shape[0]
    for k, third in enumerate((own, above, below)):
        at = zl_ref[0] + k
        at = jnp.where(at >= NZL, at - NZL, at)
        out[pl.ds(at * size, size)] = third[...]


def in_z_order(zl, own, above, below, after):
    vmem = pl.BlockSpec(memory_space=pltpu.VMEM)
    return pl.pallas_call(
        thirds_kernel,
        out_shape=jax.ShapeDtypeStruct((NZL * own.shape[0], *own.shape[1:]), BF),
        in_specs=[pl.BlockSpec(memory_space=pltpu.SMEM), vmem, vmem, vmem, pl.BlockSpec(memory_space=pl.ANY)],
        out_specs=vmem,
        compiler_params=pltpu.CompilerParams(vmem_limit_bytes=60 * 2**20),
        cost_estimate=pl.CostEstimate(flops=0, bytes_accessed=4 * NZL * own.size, transcendentals=0),
    )(zl, own, above, below, after)


def adam_kernel(terms, master, first, second, after, new_first, new_second, new_weight):
    half = terms.shape[-1]
    total = jnp.sum(terms[...].astype(F32), axis=0)
    for k in range(NC):
        at = slice(k * half, (k + 1) * half)
        gradient = total[k]
        one = BETA_ONE * first[:, at] + (1.0 - BETA_ONE) * gradient
        two = BETA_TWO * second[:, at] + (1.0 - BETA_TWO) * gradient * gradient
        new_first[:, at] = one
        new_second[:, at] = two
        new_weight[:, at] = master[:, at] - STEP_SIZE * (
            one / CORRECT_ONE / (jnp.sqrt(two / CORRECT_TWO) + EPSILON)
        )


def adam(terms, master, first, second, after):
    vmem = pl.BlockSpec(memory_space=pltpu.VMEM)
    shape = jax.ShapeDtypeStruct(master.shape, F32)
    return pl.pallas_call(
        adam_kernel,
        out_shape=(shape, shape, shape),
        in_specs=[vmem] * 4 + [pl.BlockSpec(memory_space=pl.ANY)],
        out_specs=(vmem, vmem, vmem),
        compiler_params=pltpu.CompilerParams(vmem_limit_bytes=60 * 2**20),
        cost_estimate=pl.CostEstimate(flops=20 * master.size, bytes_accessed=24 * master.size + 2 * terms.size, transcendentals=0),
    )(terms, master, first, second, after)


def term_kernel(plan, where, tokens, theirs, cot, cot_theirs, after, *rest):
    outs, (lhs, rhs, sems) = rest[: len(plan)], rest[len(plan) :]
    rows, chunk = lhs.shape[1] // 2, lhs.shape[2]
    half = outs[0].shape[1]
    chunks = sorted({p[0] for p in plan})

    def copies(k):
        columns = pl.ds(pl.multiple_of(where[chunks[k]] * chunk, 128), chunk)
        return [
            pltpu.make_async_copy(source.at[:, columns], lhs.at[k, pl.ds(d * rows, rows)], sems.at[k, d])
            for d, source in enumerate((tokens, theirs))
        ]

    for k in range(len(chunks)):
        for copy in copies(k):
            copy.start()
    arrived = set()
    for out, (which, side, kind) in zip(outs, plan):
        columns = pl.ds(pl.multiple_of(where[side] * half, 128), half)
        rhs[:rows] = cot[:, columns]
        rhs[rows:] = cot_theirs[:, columns]
        k = chunks.index(which)
        if k not in arrived:
            arrived.add(k)
            for copy in copies(k):
                copy.wait()
        value = lax.dot_general(lhs[k], rhs[...], (((0,), (0,)), ((), ())), preferred_element_type=F32)
        out[...] = value.astype(kind)


def terms(plan, where, tokens, theirs, cot, cot_theirs, after):
    rows, chunk, half = tokens.shape[0], tokens.shape[1] // NX, cot.shape[1] // 2
    vmem, hbm = pl.BlockSpec(memory_space=pltpu.VMEM), pl.BlockSpec(memory_space=pl.ANY)
    count = len({p[0] for p in plan})
    return pl.pallas_call(
        functools.partial(term_kernel, plan),
        out_shape=[jax.ShapeDtypeStruct((chunk, half), p[2]) for p in plan],
        in_specs=[pl.BlockSpec(memory_space=pltpu.SMEM), hbm, hbm, vmem, vmem, hbm],
        out_specs=[vmem] * len(plan),
        scratch_shapes=[
            pltpu.VMEM((count, 2 * rows, chunk), BF),
            pltpu.VMEM((2 * rows, half), BF),
            pltpu.SemaphoreType.DMA((count, 2)),
        ],
        compiler_params=pltpu.CompilerParams(vmem_limit_bytes=60 * 2**20),
        cost_estimate=pl.CostEstimate(
            flops=4 * rows * chunk * half * len(plan), bytes_accessed=4 * rows * chunk * count, transcendentals=0
        ),
    )(where, tokens, theirs, cot, cot_theirs, after)


def local(tokens, cot, codes, scales, master, first, second):
    width, columns = tokens.shape[1], cot.shape[1]
    x, zl, c = (lax.axis_index(a).astype(jnp.uint32) for a in ("x", "zl", "c"))
    nz = NZH * NZL
    swap = [(0, 1), (1, 0)]
    z_up = [(i, (i + 1) % nz) for i in range(nz)]
    z_down = [(i, (i - 1) % nz) for i in range(nz)]

    theirs = lax.ppermute(tokens, "c", swap)
    cot_theirs = lax.ppermute(cot, "c", swap)

    w = (codes.astype(F32) * scales.astype(F32)).astype(BF)
    below = lax.ppermute(w, ("zh", "zl"), z_up)
    above = lax.ppermute(w, ("zh", "zl"), z_down)

    chunk, half = width // NX, columns // 2
    on = x + 1 + 2 * c

    where = jnp.stack([(x + 2) & (NX - 1), on & (NX - 1), x, c, 1 - c]).astype(jnp.int32)
    both = (where, tokens, theirs, cot, cot_theirs)
    TWO, ONE, HERE, NEAR, FAR = range(5)
    straight = [(2 * i + d, 2 * ((i + 1 - 2 * d) % NX) + d) for i in range(NX) for d in range(2)]
    crossed = [(2 * i + d, 2 * ((i + 1 - 2 * d) % NX) + 1 - d) for i in range(NX) for d in range(2)]
    (two_on,) = terms([(TWO, NEAR, BF)], *both, cot)
    tiles = in_z_order(zl.astype(jnp.int32).reshape(1), w, above, below, two_on)
    tiles = lax.all_gather(tiles, ("y", "c"), axis=0)
    (one_far,) = terms([(ONE, FAR, BF)], *both, two_on)
    (one_near,) = terms([(ONE, NEAR, F32)], *both, one_far)
    two_on = lax.ppermute(two_on, ("x", "c"), straight)
    one_far = lax.ppermute(one_far, ("x", "c"), crossed)
    one_near = (one_near + two_on.astype(F32)).astype(BF)
    (here,) = terms([(HERE, NEAR, F32)], *both, one_near)
    one_near = lax.ppermute(one_near, ("x", "c"), straight)
    summed = (here + one_far.astype(F32) + one_near.astype(F32)).astype(BF)

    rows = chunk // (nz * NY)
    thirds = summed.reshape(NZH, NZL, NY * rows, half)

    def third(j):
        return lax.dynamic_index_in_dim(thirds, jnp.where(j > 2, j - 3, j), axis=1, keepdims=False)

    up = lax.ppermute(third(zl + 1), ("zh", "zl"), z_up)
    down = lax.ppermute(third(zl + 2), ("zh", "zl"), z_down)
    by_z = (third(zl).astype(F32) + up.astype(F32) + down.astype(F32)).astype(BF)
    last = by_z.reshape(NZH * NY * NC, rows // NC, half)
    last = lax.all_to_all(last, ("zh", "y", "c"), 0, 0, tiled=True)
    last = last.reshape(NZH * NY, NC, rows // NC, half)

    projected = project(tokens, tiles, columns)
    return projected, *adam(last, master, first, second, projected)


def solution(mesh):
    fine = Mesh(mesh.devices.reshape(NX, NZH, NZL, NY, NC), AXES)
    rows = P(AXES, None)
    tiles = P(("zl", "y", "c"), None, None)
    return jax.shard_map(
        local,
        mesh=fine,
        in_specs=(rows, rows, tiles, tiles, rows, rows, rows),
        out_specs=(rows, rows, rows, rows),
        check_vma=False,
    )
```
